32 devices in a mesh: dp: 2 (over x), ctx: 8 (over z, y), head: 2 (over core).
Axes of the slice: x: 2, y: 2, z: 4, core: 2. Of those that a mesh axis runs over, the one named last changes fastest.
Arguments:
- queries: bfloat16 [4096, 32, 128], P(('dp', 'ctx'), 'head'), parts along dimension 0, may hold values from -112 to 112, as said below
- keys: bfloat16 [4096, 16, 128], P(('dp', 'ctx'), 'head'), parts along dimension 0, may hold values from -4 to 4, as said below
- values: bfloat16 [4096, 16, 128], P(('dp', 'ctx'), 'head'), parts along dimension 0, may hold values from -4 to 4
- out_grad: bfloat16 [4096, 32, 128], P(('dp', 'ctx'), 'head'), parts along dimension 0, may hold values from -4 to 4
- doc_lengths: int32 [32], P('dp'), parts along dimension 0, may hold values from 1 to 512, 2048 in all
Outputs:
- attended: bfloat16 [4096, 32, 128], P(('dp', 'ctx'), 'head'), parts along dimension 0
- query_grad: bfloat16 [4096, 32, 128], P(('dp', 'ctx'), 'head'), parts along dimension 0
- key_grad: bfloat16 [4096, 16, 128], P(('dp', 'ctx'), 'head'), parts along dimension 0
- value_grad: bfloat16 [4096, 16, 128], P(('dp', 'ctx'), 'head'), parts along dimension 0
The draws below stay inside these ranges and needn't reach their ends.
There are 2 independent parts, one for each index of `dp`. The reference program is written for one: setup_inputs(seed, part) draws one part's arguments, and reference() takes and returns one part's arrays. A program takes and returns all parts, laid end to end along the dimension named above; each array names one. Nothing has to cross between parts.
Inputs may be any that keep to these rules, and one draw needn't show every extreme that they name: Entries of the queries lie in this range. Entries of the keys lie in this range. `doc_lengths`: the lengths sum to 2048; the longest document has exactly 512 tokens.
All inputs are finite; a program needn't handle non-finite values.
Results may differ from the reference program's by a relative error of at most 0.0055.
Values may be sent and summed in bfloat16 or wider, within the bound.
A program may use at most 192 MiB of HBM per device.

```python
import math
import jax
import jax.numpy as jnp
import numpy as np
from jax import lax

HEADS = 32
KV_HEADS = 16
HEAD_DIM = 128
WINDOW = 1024
TOK_DEV = 256
GROUP = 2
REACH = 4
ROW = 2048
DOCS = 16


def shared_keys(key):
    base_keys = jnp.clip(jax.random.normal(jax.random.fold_in(key, 21), (ROW, KV_HEADS, HEAD_DIM), jnp.float32), -4.0, 4.0)
    return base_keys


def draw_keys(key, part):
    base_keys = shared_keys(key)
    return base_keys.astype(jnp.bfloat16)


def draw_queries(key, part):
    drawn = jnp.clip(jax.random.normal(jax.random.fold_in(key, 31), (ROW, HEADS, HEAD_DIM), jnp.float32), -4.0, 4.0)
    return drawn.astype(jnp.bfloat16)


def levels(stream_key, dims, pieces, smallest, high):
    def one(position, shards_of):
        draws = jax.random.uniform(jax.random.fold_in(jax.random.fold_in(stream_key, 6), position), (shards_of,), jnp.float32, smallest / len(pieces), high / len(pieces))
        return jnp.repeat(jnp.exp(draws), dims[position] // shards_of).reshape((-1,) + (1,) * (len(dims) - position - 1))

    level = one(*pieces[0])
    for cut in pieces[1:]:
        level = level * one(*cut)
    return level


def profile(number_of, total, most, skew):
    portions = [(1 << 20) // math.isqrt(grade ** skew) + 1 for grade in range(2, number_of + 1)]
    spare, counts = total - most - (number_of - 1), [1] * (number_of - 1)
    while spare > 0:
        candidates = [i for i in range(number_of - 1) if counts[i] < most]
        whole, left = sum([portions[i] for i in candidates]), spare
        for i in candidates:
            extra = min(most - counts[i], max(1, left * portions[i] // whole), spare)
            counts[i] = counts[i] + extra
            spare = spare - extra
    return np.array([most] + counts)


def ragged(key, number_of, total, most, lean):
    if number_of == 2:
        one = jax.random.randint(key, (), max(1, total - most), min(most, total - 1) + 1)
        return jnp.stack([one, total - one])
    tallies = jnp.asarray(profile(number_of, total, most, lean), jnp.int32)
    couples = (number_of - 1) // 2
    source_of, sink = tallies[1:1 + 2 * couples:2], tallies[2:2 + 2 * couples:2]
    margin = jnp.minimum(source_of - 1, most - sink)
    moved = jax.random.randint(jax.random.fold_in(key, 1), (couples,), 0, 1 << 20) % (margin + 1)
    tallies = tallies.at[1:1 + 2 * couples:2].set(source_of - moved).at[2:2 + 2 * couples:2].set(sink + moved)
    return tallies[jax.random.permutation(jax.random.fold_in(key, 2), number_of)]


def normal_values(key, dims, deviation, reach, pieces=(), kind=jnp.bfloat16):
    level = levels(key, dims, pieces, -0.22, 0.18) if pieces else 1.0
    entries = jax.random.normal(key, dims, jnp.float32) * deviation * level
    return jnp.minimum(jnp.maximum(entries, -reach), reach).astype(kind)


def setup_inputs(seed: int = 0, part: int = 0) -> dict:
    seeds = jax.random.split(jax.random.key(seed), 6)
    own_keys = jax.random.split(jax.random.fold_in(seeds[5], part), 6)
    queries = draw_queries(jax.random.fold_in(jax.random.fold_in(seeds[5], part), 71), part)
    keys = draw_keys(jax.random.fold_in(jax.random.fold_in(seeds[5], part), 71), part)
    values = normal_values(own_keys[2], (ROW, KV_HEADS, HEAD_DIM), 1.0, 4.0, ((0, 8), (1, 2)))
    out_grad = normal_values(own_keys[3], (ROW, HEADS, HEAD_DIM), 1.0, 4.0, ((0, 8), (1, 2)))
    doc_lengths = ragged(own_keys[4], DOCS, ROW, ROW // 4, 2).astype(jnp.int32)
    return dict(queries=queries, keys=keys, values=values, out_grad=out_grad, doc_lengths=doc_lengths)


SCALING = 168.0 ** -0.5


def doc_index(positions, doc_lengths):
    ends = jnp.cumsum(doc_lengths).astype(jnp.int32)
    return jnp.sum((positions[:, None] >= ends[None, :]).astype(jnp.int32), axis=1)


def reference(queries, keys, values, out_grad, doc_lengths):
    row_length = queries.shape[0]
    halo_rows = REACH * TOK_DEV
    key_span = halo_rows + TOK_DEV
    padding = jnp.zeros((halo_rows, KV_HEADS, HEAD_DIM), keys.dtype)
    keys_padded = jnp.concatenate([padding, keys], 0)
    values_padded = jnp.concatenate([padding, values], 0)
    blocks = row_length // TOK_DEV

    def advance(running, block_index):
        key_acc, value_acc = running
        offset = (block_index * TOK_DEV).astype(jnp.int32)
        query_block = lax.dynamic_slice_in_dim(queries, offset, TOK_DEV, 0).astype(jnp.float32).reshape(TOK_DEV, KV_HEADS, GROUP, HEAD_DIM)
        grad_block = lax.dynamic_slice_in_dim(out_grad, offset, TOK_DEV, 0).astype(jnp.float32).reshape(TOK_DEV, KV_HEADS, GROUP, HEAD_DIM)
        key_block = lax.dynamic_slice_in_dim(keys_padded, offset, key_span, 0).astype(jnp.float32)
        value_block = lax.dynamic_slice_in_dim(values_padded, offset, key_span, 0).astype(jnp.float32)
        query_pos = offset + jnp.arange(TOK_DEV, dtype=jnp.int32)
        key_pos = offset - halo_rows + jnp.arange(key_span, dtype=jnp.int32)
        gap = query_pos[:, None] - key_pos[None, :]
        allowed = (gap >= 0) & (gap < WINDOW) & (key_pos[None, :] >= 0)
        allowed = allowed & (doc_index(query_pos, doc_lengths)[:, None] == doc_index(key_pos, doc_lengths)[None, :])
        scores = SCALING * jnp.einsum("qgjd,kgd->gjqk", query_block, key_block)
        maximum = jnp.max(jnp.where(allowed, scores, -jnp.inf), axis=3, keepdims=True)
        weights = jnp.where(allowed, jnp.exp(scores - maximum), 0.0)
        weights = weights / jnp.sum(weights, axis=3, keepdims=True)
        rounded = lax.optimization_barrier(weights.astype(jnp.bfloat16)).astype(jnp.float32)
        attended = jnp.einsum("gjqk,kgd->qgjd", rounded, value_block).astype(jnp.bfloat16)
        weight_grad = jnp.einsum("qgjd,kgd->gjqk", grad_block, value_block)
        row_total = jnp.sum(weights * weight_grad, axis=3, keepdims=True)
        score_grad = lax.optimization_barrier((weights * (weight_grad - row_total)).astype(jnp.bfloat16)).astype(jnp.float32)
        query_grad = (SCALING * jnp.einsum("gjqk,kgd->qgjd", score_grad, key_block)).astype(jnp.bfloat16)
        key_part = SCALING * jnp.einsum("gjqk,qgjd->kgd", score_grad, query_block)
        value_part = jnp.einsum("gjqk,qgjd->kgd", rounded, grad_block)
        key_acc = lax.dynamic_update_slice_in_dim(key_acc, lax.dynamic_slice_in_dim(key_acc, offset, key_span, 0) + key_part, offset, 0)
        value_acc = lax.dynamic_update_slice_in_dim(value_acc, lax.dynamic_slice_in_dim(value_acc, offset, key_span, 0) + value_part, offset, 0)
        return (key_acc, value_acc), (attended.reshape(TOK_DEV, HEADS, HEAD_DIM), query_grad.reshape(TOK_DEV, HEADS, HEAD_DIM))

    start_acc = jnp.zeros((halo_rows + row_length, KV_HEADS, HEAD_DIM), jnp.float32)
    (key_acc, value_acc), (attended, query_grad) = lax.scan(advance, (start_acc, start_acc), jnp.arange(blocks, dtype=jnp.int32))
    attended = attended.reshape(row_length, HEADS, HEAD_DIM)
    query_grad = query_grad.reshape(row_length, HEADS, HEAD_DIM)
    key_grad = key_acc[halo_rows:].astype(jnp.bfloat16)
    value_grad = value_acc[halo_rows:].astype(jnp.bfloat16)
    return (attended, query_grad, key_grad, value_grad)
```

```python
import functools

import jax
import jax.numpy as jnp
from jax import lax
from jax.experimental import pallas as pl
from jax.experimental.pallas import tpu as pltpu
from jax.sharding import PartitionSpec as P

WINDOW = 1024
SCALING = 168.0 ** (-0.5)
LOG2E = 1.4426950408889634
MASKED = -1e30
MESH = pl.DeviceIdType.MESH
F32 = jnp.float32
BF16 = jnp.bfloat16


def kernel(
    size, reach, doc_ref, q_ref, g_ref, k_ref, v_ref,
    out_ref, dq_ref, dk_ref, dv_ref,
    k_all, v_all, k_own, v_own, k_part, v_part, k_back, v_back, bias,
    kv_send, kv_recv, grad_send, grad_recv,
):
    groups, rows, dim = k_ref.shape
    span = (reach + 1) * rows
    me = lax.axis_index("ctx")
    distances = range(1, reach + 1)

    def slot(d):
        return pl.ds((reach - d) * rows, rows)

    def outward(d, g, which):
        src, dst = ((k_ref, k_all), (v_ref, v_all))[which]
        return pltpu.make_async_remote_copy(
            src_ref=src.at[g],
            dst_ref=dst.at[g, slot(d)],
            send_sem=kv_send.at[d - 1, which, g],
            recv_sem=kv_recv.at[d - 1, which, g],
            device_id={"ctx": me + d},
            device_id_type=MESH,
        )

    def backward(d, g, which):
        src, dst = ((k_part, k_back), (v_part, v_back))[which]
        return pltpu.make_async_remote_copy(
            src_ref=src.at[d - 1, g],
            dst_ref=dst.at[d - 1, g],
            send_sem=grad_send.at[d - 1, which, g],
            recv_sem=grad_recv.at[d - 1, which, g],
            device_id={"ctx": me - d},
            device_id_type=MESH,
        )

    barrier = pltpu.get_barrier_semaphore()
    for d in distances:
        @pl.when(me + d < size)
        def _():
            pl.semaphore_signal(barrier, inc=1, device_id={"ctx": me + d}, device_id_type=MESH)

        @pl.when(me >= d)
        def _():
            pl.semaphore_signal(barrier, inc=1, device_id={"ctx": me - d}, device_id_type=MESH)

    peers = jnp.minimum(me, reach) + jnp.minimum(size - 1 - me, reach)
    pl.semaphore_wait(barrier, peers)

    @pl.loop(0, groups)
    def _(g):
        for d in distances:
            @pl.when(me + d < size)
            def _():
                for which in range(2):
                    outward(d, g, which).start()

    lane = lax.broadcasted_iota(jnp.int32, (1, rows), 1)
    position = me * rows + lane
    first = jnp.maximum(position - (WINDOW - 1), 0)
    end = jnp.int32(0)
    for n in range(doc_ref.shape[0]):
        end = end + doc_ref[n]
        first = jnp.maximum(first, jnp.where(position >= end, end, 0))
    first = first - (me - reach) * rows
    at = lax.broadcasted_iota(jnp.int32, (span, rows), 0)
    seen = (at >= first) & (at <= lane + reach * rows)
    mask = jnp.where(seen, 0.0, MASKED).astype(F32)
    bias[:, :rows] = mask
    bias[:, rows:] = mask

    k_all[:, slot(0), :] = k_ref[...]
    v_all[:, slot(0), :] = v_ref[...]
    for d in distances:
        @pl.when(me < d)
        def _():
            k_all[:, slot(d), :] = jnp.zeros((groups, rows, dim), BF16)
            v_all[:, slot(d), :] = jnp.zeros((groups, rows, dim), BF16)

    def across(left, right):
        return lax.dot_general(left, right, (((1,), (1,)), ((), ())), preferred_element_type=F32)

    def product(left, right):
        return jnp.dot(left, right, preferred_element_type=F32)

    def flipped(array):
        return array.astype(F32).T.astype(BF16)

    @pl.loop(0, groups)
    def _(g):
        for d in distances:
            @pl.when(me >= d)
            def _():
                for which in range(2):
                    outward(d, g, which).wait_recv()

        query, grad, key, value = q_ref[g], g_ref[g], k_all[g], v_all[g]
        scores = across(key, query) * (SCALING * LOG2E) + bias[...]
        expo = jnp.exp2(scores - jnp.max(scores, axis=0, keepdims=True))
        weights = expo * (1.0 / jnp.sum(expo, axis=0, keepdims=True))
        rounded = weights.astype(BF16)
        weight_grad = across(value, grad)
        row_total = jnp.sum(weights * weight_grad, axis=0, keepdims=True)
        score_grad = (weights * (weight_grad - row_total)).astype(BF16)
        key_grad = product(score_grad, query) * SCALING
        value_grad = product(rounded, grad)
        k_own[g] = key_grad[reach * rows:]
        v_own[g] = value_grad[reach * rows:]
        for d in distances:
            low = (reach - d) * rows
            k_part[d - 1, g] = key_grad[low:low + rows].astype(BF16)
            v_part[d - 1, g] = value_grad[low:low + rows].astype(BF16)

            @pl.when(me >= d)
            def _():
                for which in range(2):
                    backward(d, g, which).start()

        out_ref[g] = product(flipped(value), rounded).T.astype(BF16)
        dq_ref[g] = (product(flipped(key), score_grad) * SCALING).T.astype(BF16)

    @pl.loop(0, groups)
    def _(g):
        for d in distances:
            @pl.when(me + d < size)
            def _():
                for which in range(2):
                    backward(d, g, which).wait_recv()
                k_own[g] += k_back[d - 1, g].astype(F32)
                v_own[g] += v_back[d - 1, g].astype(F32)

        dk_ref[g] = k_own[g].astype(BF16)
        dv_ref[g] = v_own[g].astype(BF16)

    @pl.loop(0, groups)
    def _(g):
        for d in distances:
            @pl.when(me + d < size)
            def _():
                for which in range(2):
                    outward(d, g, which).wait_send()

            @pl.when(me >= d)
            def _():
                for which in range(2):
                    backward(d, g, which).wait_send()


def body(queries, keys, values, out_grad, doc_lengths):
    rows, heads, dim = queries.shape
    groups = keys.shape[1]
    per = heads // groups
    size = lax.axis_size("ctx")
    reach = min(WINDOW, rows * size // 4) // rows
    span = (reach + 1) * rows

    def split(array):
        return array.reshape(rows, groups, per, dim).transpose(1, 2, 0, 3).reshape(groups, per * rows, dim)

    def joined(array):
        return array.reshape(groups, per, rows, dim).transpose(2, 0, 1, 3).reshape(rows, heads, dim)

    vmem = pl.BlockSpec(memory_space=pltpu.VMEM)
    dma = pltpu.SemaphoreType.DMA((reach, 2, groups))
    wide = jax.ShapeDtypeStruct((groups, per * rows, dim), BF16)
    narrow = jax.ShapeDtypeStruct((groups, rows, dim), BF16)
    out, dq, dk, dv = pl.pallas_call(
        functools.partial(kernel, size, reach),
        out_shape=(wide, wide, narrow, narrow),
        in_specs=[pl.BlockSpec(memory_space=pltpu.SMEM)] + [vmem] * 4,
        out_specs=(vmem,) * 4,
        scratch_shapes=[
            pltpu.VMEM((groups, span, dim), BF16),
            pltpu.VMEM((groups, span, dim), BF16),
            pltpu.VMEM((groups, rows, dim), F32),
            pltpu.VMEM((groups, rows, dim), F32),
            pltpu.VMEM((reach, groups, rows, dim), BF16),
            pltpu.VMEM((reach, groups, rows, dim), BF16),
            pltpu.VMEM((reach, groups, rows, dim), BF16),
            pltpu.VMEM((reach, groups, rows, dim), BF16),
            pltpu.VMEM((span, per * rows), F32),
            dma, dma, dma, dma,
        ],
        compiler_params=pltpu.CompilerParams(
            collective_id=0, has_side_effects=True, vmem_limit_bytes=56 * 2**20
        ),
    )(doc_lengths, split(queries), split(out_grad), keys.transpose(1, 0, 2), values.transpose(1, 0, 2))
    return joined(out), joined(dq), dk.transpose(1, 0, 2), dv.transpose(1, 0, 2)


def solution(mesh):
    spec = P(("dp", "ctx"), "head", None)
    return jax.shard_map(
        body,
        mesh=mesh,
        in_specs=(spec, spec, spec, spec, P("dp")),
        out_specs=(spec, spec, spec, spec),
        check_vma=False,
    )
```

```python
import functools

import jax
import jax.numpy as jnp
from jax import lax
from jax.experimental import pallas as pl
from jax.experimental.pallas import tpu as pltpu
from jax.sharding import PartitionSpec as P

WINDOW = 1024
SCALING = 168.0 ** (-0.5)
LOG2E = 1.4426950408889634
MASKED = -1e30
LAG = 2
MESH = pl.DeviceIdType.MESH
F32 = jnp.float32
BF16 = jnp.bfloat16


def kernel(
    size, reach, doc_ref, q_ref, g_ref, k_ref, v_ref,
    out_ref, dq_ref, dk_ref, dv_ref,
    q_wide, g_wide, k_wide, v_wide, out_wide, dq_wide, dk_wide, dv_wide,
    kv_all, part, back, relay, bias,
    kv_send, kv_recv, grad_send, grad_recv, relay_recv, pass_send,
):
    rows, groups, dim = k_ref.shape
    heads = q_ref.shape[1]
    per = heads // groups
    span = (reach + 1) * rows
    me = lax.axis_index("ctx")
    plane, spot = me // reach, me % reach
    planes = size // reach
    distances = range(1, reach + 1)
    near = range(1, reach)

    def slot(d):
        return pl.ds((reach - d) * rows, rows)

    def remote(src, dst, send, recv, to):
        return pltpu.make_async_remote_copy(
            src_ref=src, dst_ref=dst, send_sem=send, recv_sem=recv,
            device_id={"ctx": to}, device_id_type=MESH,
        )

    def outward(d, g):
        return remote(
            kv_all.at[g, :, slot(0)], kv_all.at[g, :, slot(d)],
            kv_send.at[d - 1, g], kv_recv.at[d - 1, g], me + d,
        )

    def passed(d, g):
        return remote(
            kv_all.at[g, :, slot(reach)], kv_all.at[g, :, slot(d)],
            pass_send.at[d - 1, g], kv_recv.at[d - 1, g], me - (reach - d),
        )

    def homeward(d, g):
        return remote(
            part.at[d - 1, g], back.at[d - 1, g],
            grad_send.at[d - 1, g], grad_recv.at[d - 1, g], me - d,
        )

    def relayed(d, g):
        return remote(
            part.at[d - 1, g], relay.at[d - 1, g],
            grad_send.at[d - 1, g], relay_recv.at[d - 1, g], me + (reach - d),
        )

    barrier = pltpu.get_barrier_semaphore()

    def greet(to):
        pl.semaphore_signal(barrier, inc=1, device_id={"ctx": to}, device_id_type=MESH)

    for o in near:
        greet(plane * reach + (spot + o) % reach)

    @pl.when(plane > 0)
    def _():
        greet(me - reach)

    @pl.when(plane < planes - 1)
    def _():
        greet(me + reach)

    k_wide[...] = k_ref[...].astype(F32).reshape(rows * groups, dim)
    v_wide[...] = v_ref[...].astype(F32).reshape(rows * groups, dim)
    peers = (reach - 1) + jnp.minimum(plane, 1) + jnp.minimum(planes - 1 - plane, 1)
    pl.semaphore_wait(barrier, peers)

    @pl.loop(0, groups)
    def _(g):
        kv_all[g, 0, slot(0), :] = k_wide[pl.ds(g, rows, stride=groups), :].astype(BF16)
        kv_all[g, 1, slot(0), :] = v_wide[pl.ds(g, rows, stride=groups), :].astype(BF16)

        @pl.when(plane < planes - 1)
        def _():
            outward(reach, g).start()

        for d in near:
            @pl.when(spot + d < reach)
            def _():
                outward(d, g).start()

    q_wide[...] = q_ref[...].astype(F32).reshape(rows * heads, dim)
    g_wide[...] = g_ref[...].astype(F32).reshape(rows * heads, dim)

    lane = lax.broadcasted_iota(jnp.int32, (1, rows), 1)
    position = me * rows + lane
    first = jnp.maximum(position - (WINDOW - 1), 0)
    end = jnp.int32(0)
    for n in range(doc_ref.shape[0]):
        end = end + doc_ref[n]
        first = jnp.maximum(first, jnp.where(position >= end, end, 0))
    first = first - (me - reach) * rows
    at = lax.broadcasted_iota(jnp.int32, (span, rows), 0)
    seen = (at >= first) & (at <= lane + reach * rows)
    mask = jnp.where(seen, 0.0, MASKED).astype(F32)
    for n in range(per):
        bias[:, n * rows:(n + 1) * rows] = mask

    for d in distances:
        @pl.when(me < d)
        def _():
            kv_all[:, :, slot(d), :] = jnp.zeros((groups, 2, rows, dim), BF16)

    def across(left, right):
        return lax.dot_general(left, right, (((1,), (1,)), ((), ())), preferred_element_type=F32)

    def product(left, right):
        return jnp.dot(left, right, preferred_element_type=F32)

    def flipped(array):
        return array.astype(F32).T.astype(BF16)

    def head_rows(wide, g):
        return jnp.concatenate(
            [wide[pl.ds(g * per + n, rows, stride=heads), :] for n in range(per)], 0
        ).astype(BF16)

    def store_heads(wide, g, array):
        for n in range(per):
            wide[pl.ds(g * per + n, rows, stride=heads), :] = array[n * rows:(n + 1) * rows]

    def send_far(g):
        @pl.when(plane > 0)
        def _():
            for d in near:
                @pl.when(spot >= reach - d)
                def _():
                    remote(
                        part.at[d - 1, g], relay.at[d - 1, g],
                        grad_send.at[d - 1, g], relay_recv.at[d - 1, g], me - (reach - d),
                    ).wait_recv()
                    total = part[reach - 1, g].astype(F32) + relay[d - 1, g].astype(F32)
                    part[reach - 1, g] = total.astype(BF16)
            homeward(reach, g).start()

    @pl.loop(0, groups)
    def _(g):
        @pl.when(plane > 0)
        def _():
            outward(reach, g).wait_recv()
            for d in near:
                @pl.when(spot >= reach - d)
                def _():
                    passed(d, g).start()

        for d in near:
            @pl.when(me >= d)
            def _():
                outward(d, g).wait_recv()

        query, grad = head_rows(q_wide, g), head_rows(g_wide, g)
        key, value = kv_all[g, 0], kv_all[g, 1]
        scores = across(key, query) * (SCALING * LOG2E) + bias[...]
        expo = jnp.exp2(scores - jnp.max(scores, axis=0, keepdims=True))
        weights = expo * (1.0 / jnp.sum(expo, axis=0, keepdims=True))
        rounded = weights.astype(BF16)
        weight_grad = across(value, grad)
        row_total = jnp.sum(weights * weight_grad, axis=0, keepdims=True)
        score_grad = (weights * (weight_grad - row_total)).astype(BF16)
        key_grad = product(score_grad, query) * SCALING
        value_grad = product(rounded, grad)
        dk_wide[pl.ds(g, rows, stride=groups), :] = key_grad[reach * rows:]
        dv_wide[pl.ds(g, rows, stride=groups), :] = value_grad[reach * rows:]
        for d in distances:
            low = (reach - d) * rows
            part[d - 1, g, 0] = key_grad[low:low + rows].astype(BF16)
            part[d - 1, g, 1] = value_grad[low:low + rows].astype(BF16)
        for d in near:
            @pl.when(spot >= d)
            def _():
                homeward(d, g).start()

            @pl.when((spot < d) & (plane > 0))
            def _():
                relayed(d, g).start()

        store_heads(out_wide, g, product(flipped(value), rounded).T)
        store_heads(dq_wide, g, (product(flipped(key), score_grad) * SCALING).T)

        @pl.when(g >= LAG)
        def _():
            send_far(g - LAG)

    @pl.loop(groups - LAG, groups)
    def _(g):
        send_far(g)

    out_ref[...] = out_wide[...].reshape(rows, heads, dim).astype(BF16)
    dq_ref[...] = dq_wide[...].reshape(rows, heads, dim).astype(BF16)

    def add_back(d, g):
        homeward(d, g).wait_recv()
        dk_wide[pl.ds(g, rows, stride=groups), :] += back[d - 1, g, 0].astype(F32)
        dv_wide[pl.ds(g, rows, stride=groups), :] += back[d - 1, g, 1].astype(F32)

    @pl.loop(0, groups)
    def _(g):
        for d in near:
            @pl.when(spot + d < reach)
            def _():
                add_back(d, g)

        @pl.when(plane < planes - 1)
        def _():
            add_back(reach, g)

    dk_ref[...] = dk_wide[...].reshape(rows, groups, dim).astype(BF16)
    dv_ref[...] = dv_wide[...].reshape(rows, groups, dim).astype(BF16)

    @pl.loop(0, groups)
    def _(g):
        @pl.when(plane < planes - 1)
        def _():
            outward(reach, g).wait_send()

        @pl.when(plane > 0)
        def _():
            homeward(reach, g).wait_send()

        for d in near:
            @pl.when(spot + d < reach)
            def _():
                outward(d, g).wait_send()

            @pl.when((plane > 0) & (spot >= reach - d))
            def _():
                passed(d, g).wait_send()

            @pl.when(me >= d)
            def _():
                homeward(d, g).wait_send()


def body(queries, keys, values, out_grad, doc_lengths):
    rows, heads, dim = queries.shape
    groups = keys.shape[1]
    size = lax.axis_size("ctx")
    reach = min(WINDOW, rows * size // 4) // rows
    span = (reach + 1) * rows
    vmem = pl.BlockSpec(memory_space=pltpu.VMEM)
    dma = pltpu.SemaphoreType.DMA((reach, groups))
    wide = jax.ShapeDtypeStruct(queries.shape, BF16)
    narrow = jax.ShapeDtypeStruct(keys.shape, BF16)
    shares = pltpu.VMEM((reach, groups, 2, rows, dim), BF16)
    return pl.pallas_call(
        functools.partial(kernel, size, reach),
        out_shape=(wide, wide, narrow, narrow),
        in_specs=[pl.BlockSpec(memory_space=pltpu.SMEM)] + [vmem] * 4,
        out_specs=(vmem,) * 4,
        scratch_shapes=[
            pltpu.VMEM((rows * heads, dim), F32),
            pltpu.VMEM((rows * heads, dim), F32),
            pltpu.VMEM((rows * groups, dim), F32),
            pltpu.VMEM((rows * groups, dim), F32),
            pltpu.VMEM((rows * heads, dim), F32),
            pltpu.VMEM((rows * heads, dim), F32),
            pltpu.VMEM((rows * groups, dim), F32),
            pltpu.VMEM((rows * groups, dim), F32),
            pltpu.VMEM((groups, 2, span, dim), BF16),
            shares, shares, shares,
            pltpu.VMEM((span, heads // groups * rows), F32),
            dma, dma, dma, dma, dma, dma,
        ],
        compiler_params=pltpu.CompilerParams(
            collective_id=0, has_side_effects=True, vmem_limit_bytes=58 * 2**20
        ),
    )(doc_lengths, queries, out_grad, keys, values)


def solution(mesh):
    spec = P(("dp", "ctx"), "head", None)
    return jax.shard_map(
        body,
        mesh=mesh,
        in_specs=(spec, spec, spec, spec, P("dp")),
        out_specs=(spec, spec, spec, spec),
        check_vma=False,
    )
```

```python
import functools

import jax
import jax.numpy as jnp
from jax import lax
from jax.experimental import pallas as pl
from jax.experimental.pallas import tpu as pltpu
from jax.sharding import PartitionSpec as P

WINDOW = 1024
SCALING = 168.0 ** (-0.5)
LOG2E = 1.4426950408889634
MASKED = -1e30
LAG = 2
MESH = pl.DeviceIdType.MESH
F32 = jnp.float32
BF16 = jnp.bfloat16


def kernel(
    size, reach, doc_ref, q_ref, g_ref, k_ref, v_ref,
    out_ref, dq_ref, dk_ref, dv_ref,
    k_own, v_own, kv_all, part, back, relay, bias,
    kv_send, kv_recv, grad_send, grad_recv, relay_recv, pass_send,
):
    groups, rows, dim = k_ref.shape
    units, lanes = q_ref.shape[1:3]
    step = rows // units
    per = lanes // step
    depth = reach * rows + step
    me = lax.axis_index("ctx")
    plane, spot = me // reach, me % reach
    planes = size // reach
    distances = range(1, reach + 1)
    near = range(1, reach)

    def slot(d):
        return pl.ds((reach - d) * rows, rows)

    def remote(src, dst, send, recv, to):
        return pltpu.make_async_remote_copy(
            src_ref=src, dst_ref=dst, send_sem=send, recv_sem=recv,
            device_id={"ctx": to}, device_id_type=MESH,
        )

    def outward(d, g):
        return remote(
            kv_all.at[g, :, slot(0)], kv_all.at[g, :, slot(d)],
            kv_send.at[d - 1, g], kv_recv.at[d - 1, g], me + d,
        )

    def passed(d, g):
        return remote(
            kv_all.at[g, :, slot(reach)], kv_all.at[g, :, slot(d)],
            pass_send.at[d - 1, g], kv_recv.at[d - 1, g], me - (reach - d),
        )

    def homeward(d, g):
        return remote(
            part.at[d - 1, g], back.at[d - 1, g],
            grad_send.at[d - 1, g], grad_recv.at[d - 1, g], me - d,
        )

    def relayed(d, g):
        return remote(
            part.at[d - 1, g], relay.at[d - 1, g],
            grad_send.at[d - 1, g], relay_recv.at[d - 1, g], me + (reach - d),
        )

    barrier = pltpu.get_barrier_semaphore()

    def greet(to):
        pl.semaphore_signal(barrier, inc=1, device_id={"ctx": to}, device_id_type=MESH)

    for o in near:
        greet(plane * reach + (spot + o) % reach)

    @pl.when(plane > 0)
    def _():
        greet(me - reach)

    @pl.when(plane < planes - 1)
    def _():
        greet(me + reach)

    peers = (reach - 1) + jnp.minimum(plane, 1) + jnp.minimum(planes - 1 - plane, 1)
    pl.semaphore_wait(barrier, peers)

    @pl.loop(0, groups)
    def _(g):
        kv_all[g, 0, slot(0), :] = k_ref[g]
        kv_all[g, 1, slot(0), :] = v_ref[g]

        @pl.when(plane < planes - 1)
        def _():
            outward(reach, g).start()

        for d in near:
            @pl.when(spot + d < reach)
            def _():
                outward(d, g).start()

    column = lax.broadcasted_iota(jnp.int32, (1, step), 1)
    at = lax.broadcasted_iota(jnp.int32, (depth, step), 0)
    for u in range(units):
        position = me * rows + u * step + column
        first = jnp.maximum(position - (WINDOW - 1), 0)
        end = jnp.int32(0)
        for n in range(doc_ref.shape[0]):
            end = end + doc_ref[n]
            first = jnp.maximum(first, jnp.where(position >= end, end, 0))
        first = first - (me - reach) * rows - u * step
        seen = (at >= first) & (at <= column + reach * rows)
        mask = jnp.where(seen, 0.0, MASKED).astype(F32)
        for n in range(per):
            bias[u, :, n * step:(n + 1) * step] = mask

    for d in distances:
        @pl.when(me < d)
        def _():
            kv_all[:, :, slot(d), :] = jnp.zeros((groups, 2, rows, dim), BF16)

    def across(left, right):
        return lax.dot_general(left, right, (((1,), (1,)), ((), ())), preferred_element_type=F32)

    def product(left, right):
        return jnp.dot(left, right, preferred_element_type=F32)

    def flipped(array):
        return array.astype(F32).T.astype(BF16)

    def send_far(g):
        @pl.when(plane > 0)
        def _():
            for d in near:
                @pl.when(spot >= reach - d)
                def _():
                    remote(
                        part.at[d - 1, g], relay.at[d - 1, g],
                        grad_send.at[d - 1, g], relay_recv.at[d - 1, g], me - (reach - d),
                    ).wait_recv()
                    total = part[reach - 1, g].astype(F32) + relay[d - 1, g].astype(F32)
                    part[reach - 1, g] = total.astype(BF16)
            homeward(reach, g).start()

    @pl.loop(0, groups)
    def _(g):
        @pl.when(plane > 0)
        def _():
            outward(reach, g).wait_recv()
            for d in near:
                @pl.when(spot >= reach - d)
                def _():
                    passed(d, g).start()

        for d in near:
            @pl.when(me >= d)
            def _():
                outward(d, g).wait_recv()

        each = range(units)
        reached = [pl.ds(u * step, depth) for u in each]
        query = [q_ref[g, u] for u in each]
        grad = [g_ref[g, u] for u in each]
        products = [across(kv_all[g, 0, reached[u], :], query[u]) for u in each]
        weight_grad = [across(kv_all[g, 1, reached[u], :], grad[u]) for u in each]
        key_turned, value_turned = flipped(kv_all[g, 0]), flipped(kv_all[g, 1])
        key_grad, value_grad = [], []
        for u in each:
            scores = products[u] * (SCALING * LOG2E) + bias[u]
            expo = jnp.exp2(scores - jnp.max(scores, axis=0, keepdims=True))
            inverse = 1.0 / jnp.sum(expo, axis=0, keepdims=True)
            row_total = jnp.sum(expo * weight_grad[u], axis=0, keepdims=True) * inverse
            weights = expo * inverse
            rounded = weights.astype(BF16)
            score_grad = (weights * (weight_grad[u] - row_total)).astype(BF16)
            key_grad.append(product(score_grad, query[u]) * SCALING)
            value_grad.append(product(rounded, grad[u]))
            low = u * step
            out_ref[g, u] = product(value_turned[:, low:low + depth], rounded).T.astype(BF16)
            turned = product(key_turned[:, low:low + depth], score_grad) * SCALING
            dq_ref[g, u] = turned.T.astype(BF16)

        def total(shares, low):
            found = [
                share[low - u * step:low - u * step + step]
                for u, share in enumerate(shares)
                if 0 <= low - u * step < depth
            ]
            return functools.reduce(jnp.add, found)

        for n in range(units):
            inner = slice(n * step, (n + 1) * step)
            k_own[g, inner] = total(key_grad, reach * rows + n * step)
            v_own[g, inner] = total(value_grad, reach * rows + n * step)
            for d in distances:
                low = (reach - d) * rows + n * step
                part[d - 1, g, 0, inner] = total(key_grad, low).astype(BF16)
                part[d - 1, g, 1, inner] = total(value_grad, low).astype(BF16)
        for d in near:
            @pl.when(spot >= d)
            def _():
                homeward(d, g).start()

            @pl.when((spot < d) & (plane > 0))
            def _():
                relayed(d, g).start()

        @pl.when(g >= LAG)
        def _():
            send_far(g - LAG)

    @pl.loop(groups - LAG, groups)
    def _(g):
        send_far(g)

    def add_back(d, g):
        homeward(d, g).wait_recv()
        k_own[g] += back[d - 1, g, 0].astype(F32)
        v_own[g] += back[d - 1, g, 1].astype(F32)

    @pl.loop(0, groups)
    def _(g):
        for d in near:
            @pl.when(spot + d < reach)
            def _():
                add_back(d, g)

        @pl.when(plane < planes - 1)
        def _():
            add_back(reach, g)

        dk_ref[g] = k_own[g].astype(BF16)
        dv_ref[g] = v_own[g].astype(BF16)

    @pl.loop(0, groups)
    def _(g):
        @pl.when(plane < planes - 1)
        def _():
            outward(reach, g).wait_send()

        @pl.when(plane > 0)
        def _():
            homeward(reach, g).wait_send()

        for d in near:
            @pl.when(spot + d < reach)
            def _():
                outward(d, g).wait_send()

            @pl.when((plane > 0) & (spot >= reach - d))
            def _():
                passed(d, g).wait_send()

            @pl.when(me >= d)
            def _():
                homeward(d, g).wait_send()


def body(queries, keys, values, out_grad, doc_lengths):
    rows, heads, dim = queries.shape
    groups = keys.shape[1]
    per = heads // groups
    step = 128
    units = rows // step
    size = lax.axis_size("ctx")
    reach = min(WINDOW, rows * size // 4) // rows
    span = (reach + 1) * rows

    def split(array):
        array = array.reshape(units, step, groups, per, dim).transpose(2, 0, 3, 1, 4)
        return array.reshape(groups, units, per * step, dim)

    def joined(array):
        array = array.reshape(groups, units, per, step, dim).transpose(1, 3, 0, 2, 4)
        return array.reshape(rows, heads, dim)

    vmem = pl.BlockSpec(memory_space=pltpu.VMEM)
    dma = pltpu.SemaphoreType.DMA((reach, groups))
    wide = jax.ShapeDtypeStruct((groups, units, per * step, dim), BF16)
    narrow = jax.ShapeDtypeStruct((groups, rows, dim), BF16)
    shares = pltpu.VMEM((reach, groups, 2, rows, dim), BF16)
    out, dq, dk, dv = pl.pallas_call(
        functools.partial(kernel, size, reach),
        out_shape=(wide, wide, narrow, narrow),
        in_specs=[pl.BlockSpec(memory_space=pltpu.SMEM)] + [vmem] * 4,
        out_specs=(vmem,) * 4,
        scratch_shapes=[
            pltpu.VMEM((groups, rows, dim), F32),
            pltpu.VMEM((groups, rows, dim), F32),
            pltpu.VMEM((groups, 2, span, dim), BF16),
            shares, shares, shares,
            pltpu.VMEM((units, reach * rows + step, per * step), F32),
            dma, dma, dma, dma, dma, dma,
        ],
        compiler_params=pltpu.CompilerParams(
            collective_id=0, has_side_effects=True, vmem_limit_bytes=48 * 2**20
        ),
    )(doc_lengths, split(queries), split(out_grad), keys.transpose(1, 0, 2), values.transpose(1, 0, 2))
    return joined(out), joined(dq), dk.transpose(1, 0, 2), dv.transpose(1, 0, 2)


def solution(mesh):
    spec = P(("dp", "ctx"), "head", None)
    return jax.shard_map(
        body,
        mesh=mesh,
        in_specs=(spec, spec, spec, spec, P("dp")),
        out_specs=(spec, spec, spec, spec),
        check_vma=False,
    )
```

```python
import functools

import jax
import jax.numpy as jnp
from jax import lax
from jax.experimental import pallas as pl
from jax.experimental.pallas import tpu as pltpu
from jax.sharding import PartitionSpec as P

WINDOW = 1024
SCALING = 168.0 ** (-0.5)
LOG2E = 1.4426950408889634
MASKED = -1e30
MESH = pl.DeviceIdType.MESH
F32 = jnp.float32
BF16 = jnp.bfloat16


def kernel(
    size, reach, doc_ref, q_ref, g_ref, k_ref, v_ref,
    out_ref, dq_ref, dk_ref, dv_ref,
    k_own, v_own, kv_all, part, back, bias,
    kv_send, kv_recv, grad_send, grad_recv,
):
    groups, rows, dim = k_ref.shape
    units, lanes = q_ref.shape[1:3]
    step = rows // units
    per = lanes // step
    depth = reach * rows + step
    me = lax.axis_index("ctx")
    distances = range(1, reach + 1)

    def slot(d):
        return pl.ds((reach - d) * rows, rows)

    def remote(src, dst, send, recv, to):
        return pltpu.make_async_remote_copy(
            src_ref=src, dst_ref=dst, send_sem=send, recv_sem=recv,
            device_id={"ctx": to}, device_id_type=MESH,
        )

    def outward(d, g):
        return remote(
            kv_all.at[g, :, slot(0)], kv_all.at[g, :, slot(d)],
            kv_send.at[d - 1, g], kv_recv.at[d - 1, g], me + d,
        )

    def homeward(d, g):
        return remote(
            part.at[d - 1, g], back.at[d - 1, g],
            grad_send.at[d - 1, g], grad_recv.at[d - 1, g], me - d,
        )

    barrier = pltpu.get_barrier_semaphore()

    for d in distances:
        @pl.when(me + d < size)
        def _():
            pl.semaphore_signal(barrier, inc=1, device_id={"ctx": me + d}, device_id_type=MESH)

        @pl.when(me >= d)
        def _():
            pl.semaphore_signal(barrier, inc=1, device_id={"ctx": me - d}, device_id_type=MESH)

    peers = jnp.minimum(me, reach) + jnp.minimum(size - 1 - me, reach)
    pl.semaphore_wait(barrier, peers)

    @pl.loop(0, groups)
    def _(g):
        kv_all[g, 0, slot(0), :] = k_ref[g]
        kv_all[g, 1, slot(0), :] = v_ref[g]

        for d in distances:
            @pl.when(me + d < size)
            def _():
                outward(d, g).start()

    column = lax.broadcasted_iota(jnp.int32, (1, step), 1)
    at = lax.broadcasted_iota(jnp.int32, (depth, step), 0)
    for u in range(units):
        position = me * rows + u * step + column
        first = jnp.maximum(position - (WINDOW - 1), 0)
        end = jnp.int32(0)
        for n in range(doc_ref.shape[0]):
            end = end + doc_ref[n]
            first = jnp.maximum(first, jnp.where(position >= end, end, 0))
        first = first - (me - reach) * rows - u * step
        seen = (at >= first) & (at <= column + reach * rows)
        mask = jnp.where(seen, 0.0, MASKED).astype(F32)
        for n in range(per):
            bias[u, :, n * step:(n + 1) * step] = mask

    for d in distances:
        @pl.when(me < d)
        def _():
            kv_all[:, :, slot(d), :] = jnp.zeros((groups, 2, rows, dim), BF16)

    def across(left, right):
        return lax.dot_general(left, right, (((1,), (1,)), ((), ())), preferred_element_type=F32)

    def product(left, right):
        return jnp.dot(left, right, preferred_element_type=F32)

    def flipped(array):
        return array.astype(F32).T.astype(BF16)

    @pl.loop(0, groups)
    def _(g):
        for d in distances:
            @pl.when(me >= d)
            def _():
                outward(d, g).wait_recv()

        each = range(units)
        reached = [pl.ds(u * step, depth) for u in each]
        query = [q_ref[g, u] for u in each]
        grad = [g_ref[g, u] for u in each]
        products = [across(kv_all[g, 0, reached[u], :], query[u]) for u in each]
        weight_grad = [across(kv_all[g, 1, reached[u], :], grad[u]) for u in each]
        key_turned, value_turned = flipped(kv_all[g, 0]), flipped(kv_all[g, 1])
        key_grad, value_grad = [], []
        for u in each:
            scores = products[u] * (SCALING * LOG2E) + bias[u]
            expo = jnp.exp2(scores - jnp.max(scores, axis=0, keepdims=True))
            inverse = 1.0 / jnp.sum(expo, axis=0, keepdims=True)
            row_total = jnp.sum(expo * weight_grad[u], axis=0, keepdims=True) * inverse
            weights = expo * inverse
            rounded = weights.astype(BF16)
            score_grad = (weights * (weight_grad[u] - row_total)).astype(BF16)
            key_grad.append(product(score_grad, query[u]) * SCALING)
            value_grad.append(product(rounded, grad[u]))
            low = u * step
            out_ref[g, u] = product(value_turned[:, low:low + depth], rounded).T.astype(BF16)
            turned = product(key_turned[:, low:low + depth], score_grad) * SCALING
            dq_ref[g, u] = turned.T.astype(BF16)

        def total(shares, low):
            found = [
                share[low - u * step:low - u * step + step]
                for u, share in enumerate(shares)
                if 0 <= low - u * step < depth
            ]
            return functools.reduce(jnp.add, found)

        for n in range(units):
            inner = slice(n * step, (n + 1) * step)
            k_own[g, inner] = total(key_grad, reach * rows + n * step)
            v_own[g, inner] = total(value_grad, reach * rows + n * step)
            for d in distances:
                low = (reach - d) * rows + n * step
                part[d - 1, g, 0, inner] = total(key_grad, low).astype(BF16)
                part[d - 1, g, 1, inner] = total(value_grad, low).astype(BF16)
        for d in distances:
            @pl.when(me >= d)
            def _():
                homeward(d, g).start()

    def add_back(d, g):
        homeward(d, g).wait_recv()
        k_own[g] += back[d - 1, g, 0].astype(F32)
        v_own[g] += back[d - 1, g, 1].astype(F32)

    @pl.loop(0, groups)
    def _(g):
        for d in distances:
            @pl.when(me + d < size)
            def _():
                add_back(d, g)

        dk_ref[g] = k_own[g].astype(BF16)
        dv_ref[g] = v_own[g].astype(BF16)

    @pl.loop(0, groups)
    def _(g):
        for d in distances:
            @pl.when(me + d < size)
            def _():
                outward(d, g).wait_send()

            @pl.when(me >= d)
            def _():
                homeward(d, g).wait_send()


def body(queries, keys, values, out_grad, doc_lengths):
    rows, heads, dim = queries.shape
    groups = keys.shape[1]
    per = heads // groups
    step = 128
    units = rows // step
    size = lax.axis_size("ctx")
    reach = min(WINDOW, rows * size // 4) // rows
    span = (reach + 1) * rows

    def split(array):
        array = array.reshape(units, step, groups, per, dim).transpose(2, 0, 3, 1, 4)
        return array.reshape(groups, units, per * step, dim)

    def joined(array):
        array = array.reshape(groups, units, per, step, dim).transpose(1, 3, 0, 2, 4)
        return array.reshape(rows, heads, dim)

    vmem = pl.BlockSpec(memory_space=pltpu.VMEM)
    dma = pltpu.SemaphoreType.DMA((reach, groups))
    wide = jax.ShapeDtypeStruct((groups, units, per * step, dim), BF16)
    narrow = jax.ShapeDtypeStruct((groups, rows, dim), BF16)
    shares = pltpu.VMEM((reach, groups, 2, rows, dim), BF16)
    out, dq, dk, dv = pl.pallas_call(
        functools.partial(kernel, size, reach),
        out_shape=(wide, wide, narrow, narrow),
        in_specs=[pl.BlockSpec(memory_space=pltpu.SMEM)] + [vmem] * 4,
        out_specs=(vmem,) * 4,
        scratch_shapes=[
            pltpu.VMEM((groups, rows, dim), F32),
            pltpu.VMEM((groups, rows, dim), F32),
            pltpu.VMEM((groups, 2, span, dim), BF16),
            shares, shares,
            pltpu.VMEM((units, reach * rows + step, per * step), F32),
            dma, dma, dma, dma,
        ],
        compiler_params=pltpu.CompilerParams(
            collective_id=0, has_side_effects=True, vmem_limit_bytes=48 * 2**20
        ),
    )(doc_lengths, split(queries), split(out_grad), keys.transpose(1, 0, 2), values.transpose(1, 0, 2))
    return joined(out), joined(dq), dk.transpose(1, 0, 2), dv.transpose(1, 0, 2)


def solution(mesh):
    spec = P(("dp", "ctx"), "head", None)
    return jax.shard_map(
        body,
        mesh=mesh,
        in_specs=(spec, spec, spec, spec, P("dp")),
        out_specs=(spec, spec, spec, spec),
        check_vma=False,
    )
```

```python
import functools

import jax
import jax.numpy as jnp
from jax import lax
from jax.experimental import pallas as pl
from jax.experimental.pallas import tpu as pltpu
from jax.sharding import PartitionSpec as P

WINDOW = 1024
SCALING = 168.0 ** (-0.5)
LOG2E = 1.4426950408889634
MASKED = -1e30
LAG = 4
MESH = pl.DeviceIdType.MESH
F32 = jnp.float32
BF16 = jnp.bfloat16


def kernel(
    size, reach, doc_ref, q_ref, g_ref, k_ref, v_ref,
    out_ref, dq_ref, dk_ref, dv_ref,
    q_wide, g_wide, k_own, v_own, kv_all, part, back, bias,
    kv_send, kv_recv, grad_send, grad_recv,
):
    groups, rows, dim = k_ref.shape
    heads = q_ref.shape[1]
    per = heads // groups
    units, lanes = out_ref.shape[1:3]
    step = lanes // per
    depth = reach * rows + step
    me = lax.axis_index("ctx")
    distances = range(1, reach + 1)

    def slot(d):
        return pl.ds((reach - d) * rows, rows)

    def remote(src, dst, send, recv, to):
        return pltpu.make_async_remote_copy(
            src_ref=src, dst_ref=dst, send_sem=send, recv_sem=recv,
            device_id={"ctx": to}, device_id_type=MESH,
        )

    def outward(d, g):
        return remote(
            kv_all.at[g, :, slot(0)], kv_all.at[g, :, slot(d)],
            kv_send.at[d - 1, g], kv_recv.at[d - 1, g], me + d,
        )

    def homeward(d, g):
        return remote(
            part.at[d - 1, g], back.at[d - 1, g],
            grad_send.at[d - 1, g], grad_recv.at[d - 1, g], me - d,
        )

    barrier = pltpu.get_barrier_semaphore()

    for d in distances:
        @pl.when(me + d < size)
        def _():
            pl.semaphore_signal(barrier, inc=1, device_id={"ctx": me + d}, device_id_type=MESH)

        @pl.when(me >= d)
        def _():
            pl.semaphore_signal(barrier, inc=1, device_id={"ctx": me - d}, device_id_type=MESH)

    peers = jnp.minimum(me, reach) + jnp.minimum(size - 1 - me, reach)
    pl.semaphore_wait(barrier, peers)

    @pl.loop(0, groups)
    def _(g):
        kv_all[g, 0, slot(0), :] = k_ref[g]
        kv_all[g, 1, slot(0), :] = v_ref[g]

        for d in distances:
            @pl.when(me + d < size)
            def _():
                outward(d, g).start()

    q_wide[...] = q_ref[...].astype(F32).reshape(rows * heads, dim)
    g_wide[...] = g_ref[...].astype(F32).reshape(rows * heads, dim)

    column = lax.broadcasted_iota(jnp.int32, (1, step), 1)
    at = lax.broadcasted_iota(jnp.int32, (depth, step), 0)
    for u in range(units):
        position = me * rows + u * step + column
        first = jnp.maximum(position - (WINDOW - 1), 0)
        end = jnp.int32(0)
        for n in range(doc_ref.shape[0]):
            end = end + doc_ref[n]
            first = jnp.maximum(first, jnp.where(position >= end, end, 0))
        first = first - (me - reach) * rows - u * step
        seen = (at >= first) & (at <= column + reach * rows)
        mask = jnp.where(seen, 0.0, MASKED).astype(F32)
        for n in range(per):
            bias[u, :, n * step:(n + 1) * step] = mask

    for d in distances:
        @pl.when(me < d)
        def _():
            kv_all[:, :, slot(d), :] = jnp.zeros((groups, 2, rows, dim), BF16)

    def across(left, right):
        return lax.dot_general(left, right, (((1,), (1,)), ((), ())), preferred_element_type=F32)

    def product(left, right):
        return jnp.dot(left, right, preferred_element_type=F32)

    def flipped(array):
        return array.astype(F32).T.astype(BF16)

    def head_rows(wide, g, u):
        starts = [u * step * heads + g * per + n for n in range(per)]
        return jnp.concatenate(
            [wide[pl.ds(start, step, stride=heads), :] for start in starts], 0
        ).astype(BF16)

    def finish(g):
        for d in distances:
            @pl.when(me + d < size)
            def _():
                homeward(d, g).wait_recv()
                k_own[g] += back[d - 1, g, 0].astype(F32)
                v_own[g] += back[d - 1, g, 1].astype(F32)

        dk_ref[g] = k_own[g].astype(BF16)
        dv_ref[g] = v_own[g].astype(BF16)

    @pl.loop(0, groups)
    def _(g):
        for d in distances:
            @pl.when(me >= d)
            def _():
                outward(d, g).wait_recv()

        each = range(units)
        reached = [pl.ds(u * step, depth) for u in each]
        query = [head_rows(q_wide, g, u) for u in each]
        grad = [head_rows(g_wide, g, u) for u in each]
        products = [across(kv_all[g, 0, reached[u], :], query[u]) for u in each]
        weight_grad = [across(kv_all[g, 1, reached[u], :], grad[u]) for u in each]
        key_turned, value_turned = flipped(kv_all[g, 0]), flipped(kv_all[g, 1])
        key_grad, value_grad = [], []
        for u in each:
            scores = products[u] * (SCALING * LOG2E) + bias[u]
            expo = jnp.exp2(scores - jnp.max(scores, axis=0, keepdims=True))
            inverse = 1.0 / jnp.sum(expo, axis=0, keepdims=True)
            row_total = jnp.sum(expo * weight_grad[u], axis=0, keepdims=True) * inverse
            weights = expo * inverse
            rounded = weights.astype(BF16)
            score_grad = (weights * (weight_grad[u] - row_total)).astype(BF16)
            key_grad.append(product(score_grad, query[u]) * SCALING)
            value_grad.append(product(rounded, grad[u]))
            low = u * step
            out_ref[g, u] = product(value_turned[:, low:low + depth], rounded).T.astype(BF16)
            turned = product(key_turned[:, low:low + depth], score_grad) * SCALING
            dq_ref[g, u] = turned.T.astype(BF16)

        def total(shares, low):
            found = [
                share[low - u * step:low - u * step + step]
                for u, share in enumerate(shares)
                if 0 <= low - u * step < depth
            ]
            return functools.reduce(jnp.add, found)

        for n in range(units):
            inner = slice(n * step, (n + 1) * step)
            k_own[g, inner] = total(key_grad, reach * rows + n * step)
            v_own[g, inner] = total(value_grad, reach * rows + n * step)
            for d in distances:
                low = (reach - d) * rows + n * step
                part[d - 1, g, 0, inner] = total(key_grad, low).astype(BF16)
                part[d - 1, g, 1, inner] = total(value_grad, low).astype(BF16)
        for d in distances:
            @pl.when(me >= d)
            def _():
                homeward(d, g).start()

        @pl.when(g >= LAG)
        def _():
            finish(g - LAG)

    @pl.loop(groups - LAG, groups)
    def _(g):
        finish(g)

    @pl.loop(0, groups)
    def _(g):
        for d in distances:
            @pl.when(me + d < size)
            def _():
                outward(d, g).wait_send()

            @pl.when(me >= d)
            def _():
                homeward(d, g).wait_send()


def body(queries, keys, values, out_grad, doc_lengths):
    rows, heads, dim = queries.shape
    groups = keys.shape[1]
    per = heads // groups
    step = 128
    units = rows // step
    size = lax.axis_size("ctx")
    reach = min(WINDOW, rows * size // 4) // rows
    span = (reach + 1) * rows

    def joined(array):
        array = array.reshape(groups, units, per, step, dim).transpose(1, 3, 0, 2, 4)
        return array.reshape(rows, heads, dim)

    vmem = pl.BlockSpec(memory_space=pltpu.VMEM)
    dma = pltpu.SemaphoreType.DMA((reach, groups))
    wide = jax.ShapeDtypeStruct((groups, units, per * step, dim), BF16)
    narrow = jax.ShapeDtypeStruct((groups, rows, dim), BF16)
    shares = pltpu.VMEM((reach, groups, 2, rows, dim), BF16)
    out, dq, dk, dv = pl.pallas_call(
        functools.partial(kernel, size, reach),
        out_shape=(wide, wide, narrow, narrow),
        in_specs=[pl.BlockSpec(memory_space=pltpu.SMEM)] + [vmem] * 4,
        out_specs=(vmem,) * 4,
        scratch_shapes=[
            pltpu.VMEM((rows * heads, dim), F32),
            pltpu.VMEM((rows * heads, dim), F32),
            pltpu.VMEM((groups, rows, dim), F32),
            pltpu.VMEM((groups, rows, dim), F32),
            pltpu.VMEM((groups, 2, span, dim), BF16),
            shares, shares,
            pltpu.VMEM((units, reach * rows + step, per * step), F32),
            dma, dma, dma, dma,
        ],
        compiler_params=pltpu.CompilerParams(
            collective_id=0, has_side_effects=True, vmem_limit_bytes=48 * 2**20
        ),
    )(doc_lengths, queries, out_grad, keys.transpose(1, 0, 2), values.transpose(1, 0, 2))
    return joined(out), joined(dq), dk.transpose(1, 0, 2), dv.transpose(1, 0, 2)


def solution(mesh):
    spec = P(("dp", "ctx"), "head", None)
    return jax.shard_map(
        body,
        mesh=mesh,
        in_specs=(spec, spec, spec, spec, P("dp")),
        out_specs=(spec, spec, spec, spec),
        check_vma=False,
    )
```

```python
import functools

import jax
import jax.numpy as jnp
from jax import lax
from jax.experimental import pallas as pl
from jax.experimental.pallas import tpu as pltpu
from jax.sharding import PartitionSpec as P

WINDOW = 1024
SCALING = 168.0 ** (-0.5)
LOG2E = 1.4426950408889634
MASKED = -1e30
LAG = 4
MESH = pl.DeviceIdType.MESH
F32 = jnp.float32
BF16 = jnp.bfloat16


def kernel(
    size, reach, doc_ref, q_ref, g_ref, k_ref, v_ref,
    out_ref, dq_ref, dk_ref, dv_ref,
    q_wide, g_wide, k_wide, v_wide, out_wide, dq_wide, k_own, v_own, kv_all, part, back, bias,
    kv_send, kv_recv, grad_send, grad_recv,
):
    rows, groups, dim = k_ref.shape
    heads = q_ref.shape[1]
    per = heads // groups
    step = 128
    units = rows // step
    depth = reach * rows + step
    me = lax.axis_index("ctx")
    distances = range(1, reach + 1)

    def slot(d):
        return pl.ds((reach - d) * rows, rows)

    def remote(src, dst, send, recv, to):
        return pltpu.make_async_remote_copy(
            src_ref=src, dst_ref=dst, send_sem=send, recv_sem=recv,
            device_id={"ctx": to}, device_id_type=MESH,
        )

    def outward(d, g):
        return remote(
            kv_all.at[g, :, slot(0)], kv_all.at[g, :, slot(d)],
            kv_send.at[d - 1, g], kv_recv.at[d - 1, g], me + d,
        )

    def homeward(d, g):
        return remote(
            part.at[d - 1, g], back.at[d - 1, g],
            grad_send.at[d - 1, g], grad_recv.at[d - 1, g], me - d,
        )

    barrier = pltpu.get_barrier_semaphore()

    for d in distances:
        @pl.when(me + d < size)
        def _():
            pl.semaphore_signal(barrier, inc=1, device_id={"ctx": me + d}, device_id_type=MESH)

        @pl.when(me >= d)
        def _():
            pl.semaphore_signal(barrier, inc=1, device_id={"ctx": me - d}, device_id_type=MESH)

    k_wide[...] = k_ref[...].astype(F32).reshape(rows * groups, dim)
    v_wide[...] = v_ref[...].astype(F32).reshape(rows * groups, dim)
    peers = jnp.minimum(me, reach) + jnp.minimum(size - 1 - me, reach)
    pl.semaphore_wait(barrier, peers)

    @pl.loop(0, groups)
    def _(g):
        kv_all[g, 0, slot(0), :] = k_wide[pl.ds(g, rows, stride=groups), :].astype(BF16)
        kv_all[g, 1, slot(0), :] = v_wide[pl.ds(g, rows, stride=groups), :].astype(BF16)

        for d in distances:
            @pl.when(me + d < size)
            def _():
                outward(d, g).start()

    q_wide[...] = q_ref[...].astype(F32).reshape(rows * heads, dim)
    g_wide[...] = g_ref[...].astype(F32).reshape(rows * heads, dim)

    column = lax.broadcasted_iota(jnp.int32, (1, step), 1)
    at = lax.broadcasted_iota(jnp.int32, (depth, step), 0)
    for u in range(units):
        position = me * rows + u * step + column
        first = jnp.maximum(position - (WINDOW - 1), 0)
        end = jnp.int32(0)
        for n in range(doc_ref.shape[0]):
            end = end + doc_ref[n]
            first = jnp.maximum(first, jnp.where(position >= end, end, 0))
        first = first - (me - reach) * rows - u * step
        seen = (at >= first) & (at <= column + reach * rows)
        mask = jnp.where(seen, 0.0, MASKED).astype(F32)
        for n in range(per):
            bias[u, :, n * step:(n + 1) * step] = mask

    for d in distances:
        @pl.when(me < d)
        def _():
            kv_all[:, :, slot(d), :] = jnp.zeros((groups, 2, rows, dim), BF16)

    def across(left, right):
        return lax.dot_general(left, right, (((1,), (1,)), ((), ())), preferred_element_type=F32)

    def product(left, right):
        return jnp.dot(left, right, preferred_element_type=F32)

    def flipped(array):
        return array.astype(F32).T.astype(BF16)

    def head_rows(wide, g, u):
        starts = [u * step * heads + g * per + n for n in range(per)]
        return jnp.concatenate(
            [wide[pl.ds(start, step, stride=heads), :] for start in starts], 0
        ).astype(BF16)

    def store_heads(wide, g, u, array):
        for n in range(per):
            start = u * step * heads + g * per + n
            wide[pl.ds(start, step, stride=heads), :] = array[n * step:(n + 1) * step]

    def finish(g):
        for d in distances:
            @pl.when(me + d < size)
            def _():
                homeward(d, g).wait_recv()
                k_own[g] += back[d - 1, g, 0].astype(F32)
                v_own[g] += back[d - 1, g, 1].astype(F32)

        dk_ref[g] = k_own[g].astype(BF16)
        dv_ref[g] = v_own[g].astype(BF16)

    @pl.loop(0, groups)
    def _(g):
        for d in distances:
            @pl.when(me >= d)
            def _():
                outward(d, g).wait_recv()

        each = range(units)
        reached = [pl.ds(u * step, depth) for u in each]
        query = [head_rows(q_wide, g, u) for u in each]
        grad = [head_rows(g_wide, g, u) for u in each]
        products = [across(kv_all[g, 0, reached[u], :], query[u]) for u in each]
        weight_grad = [across(kv_all[g, 1, reached[u], :], grad[u]) for u in each]
        key_turned, value_turned = flipped(kv_all[g, 0]), flipped(kv_all[g, 1])
        key_grad, value_grad = [], []
        for u in each:
            scores = products[u] * (SCALING * LOG2E) + bias[u]
            expo = jnp.exp2(scores - jnp.max(scores, axis=0, keepdims=True))
            inverse = 1.0 / jnp.sum(expo, axis=0, keepdims=True)
            row_total = jnp.sum(expo * weight_grad[u], axis=0, keepdims=True) * inverse
            weights = expo * inverse
            rounded = weights.astype(BF16)
            score_grad = (weights * (weight_grad[u] - row_total)).astype(BF16)
            key_grad.append(product(score_grad, query[u]) * SCALING)
            value_grad.append(product(rounded, grad[u]))
            low = u * step
            store_heads(out_wide, g, u, product(value_turned[:, low:low + depth], rounded).T)
            turned = product(key_turned[:, low:low + depth], score_grad) * SCALING
            store_heads(dq_wide, g, u, turned.T)

        def total(shares, low):
            found = [
                share[low - u * step:low - u * step + step]
                for u, share in enumerate(shares)
                if 0 <= low - u * step < depth
            ]
            return functools.reduce(jnp.add, found)

        for n in range(units):
            inner = slice(n * step, (n + 1) * step)
            k_own[g, inner] = total(key_grad, reach * rows + n * step)
            v_own[g, inner] = total(value_grad, reach * rows + n * step)
            for d in distances:
                low = (reach - d) * rows + n * step
                part[d - 1, g, 0, inner] = total(key_grad, low).astype(BF16)
                part[d - 1, g, 1, inner] = total(value_grad, low).astype(BF16)
        for d in distances:
            @pl.when(me >= d)
            def _():
                homeward(d, g).start()

        @pl.when(g >= LAG)
        def _():
            finish(g - LAG)

    out_ref[...] = out_wide[...].reshape(rows, heads, dim).astype(BF16)
    dq_ref[...] = dq_wide[...].reshape(rows, heads, dim).astype(BF16)

    @pl.loop(groups - LAG, groups)
    def _(g):
        finish(g)

    @pl.loop(0, groups)
    def _(g):
        for d in distances:
            @pl.when(me + d < size)
            def _():
                outward(d, g).wait_send()

            @pl.when(me >= d)
            def _():
                homeward(d, g).wait_send()


def body(queries, keys, values, out_grad, doc_lengths):
    rows, heads, dim = queries.shape
    groups = keys.shape[1]
    per = heads // groups
    step = 128
    size = lax.axis_size("ctx")
    reach = min(WINDOW, rows * size // 4) // rows
    span = (reach + 1) * rows

    vmem = pl.BlockSpec(memory_space=pltpu.VMEM)
    dma = pltpu.SemaphoreType.DMA((reach, groups))
    wide = jax.ShapeDtypeStruct(queries.shape, BF16)
    narrow = jax.ShapeDtypeStruct((groups, rows, dim), BF16)
    shares = pltpu.VMEM((reach, groups, 2, rows, dim), BF16)
    out, dq, dk, dv = pl.pallas_call(
        functools.partial(kernel, size, reach),
        out_shape=(wide, wide, narrow, narrow),
        in_specs=[pl.BlockSpec(memory_space=pltpu.SMEM)] + [vmem] * 4,
        out_specs=(vmem,) * 4,
        scratch_shapes=[
            pltpu.VMEM((rows * heads, dim), F32),
            pltpu.VMEM((rows * heads, dim), F32),
            pltpu.VMEM((rows * groups, dim), F32),
            pltpu.VMEM((rows * groups, dim), F32),
            pltpu.VMEM((rows * heads, dim), F32),
            pltpu.VMEM((rows * heads, dim), F32),
            pltpu.VMEM((groups, rows, dim), F32),
            pltpu.VMEM((groups, rows, dim), F32),
            pltpu.VMEM((groups, 2, span, dim), BF16),
            shares, shares,
            pltpu.VMEM((rows // step, reach * rows + step, per * step), F32),
            dma, dma, dma, dma,
        ],
        compiler_params=pltpu.CompilerParams(
            collective_id=0, has_side_effects=True, vmem_limit_bytes=48 * 2**20
        ),
    )(doc_lengths, queries, out_grad, keys, values)
    return out, dq, dk.transpose(1, 0, 2), dv.transpose(1, 0, 2)


def solution(mesh):
    spec = P(("dp", "ctx"), "head", None)
    return jax.shard_map(
        body,
        mesh=mesh,
        in_specs=(spec, spec, spec, spec, P("dp")),
        out_specs=(spec, spec, spec, spec),
        check_vma=False,
    )
```

```python
import functools

import jax
import jax.numpy as jnp
from jax import lax
from jax.experimental import pallas as pl
from jax.experimental.pallas import tpu as pltpu
from jax.sharding import PartitionSpec as P

WINDOW = 1024
SCALING = 168.0 ** (-0.5)
LOG2E = 1.4426950408889634
MASKED = -1e30
LAG = 4
MESH = pl.DeviceIdType.MESH
F32 = jnp.float32
BF16 = jnp.bfloat16


def kernel(
    size, reach, doc_ref, q_ref, g_ref, k_ref, v_ref,
    out_ref, dq_ref, dk_ref, dv_ref,
    q_wide, g_wide, k_own, v_own, kv_all, part, back, bias,
    kv_send, kv_recv, grad_send, grad_recv,
):
    groups, rows, dim = k_ref.shape
    heads = q_ref.shape[1]
    per = heads // groups
    units, lanes = out_ref.shape[1:3]
    step = lanes // per
    depth = reach * rows + step
    me = lax.axis_index("ctx")
    distances = range(1, reach + 1)

    def slot(d):
        return pl.ds((reach - d) * rows, rows)

    def remote(src, dst, send, recv, to):
        return pltpu.make_async_remote_copy(
            src_ref=src, dst_ref=dst, send_sem=send, recv_sem=recv,
            device_id={"ctx": to}, device_id_type=MESH,
        )

    def outward(d, g):
        return remote(
            kv_all.at[g, :, slot(0)], kv_all.at[g, :, slot(d)],
            kv_send.at[d - 1, g], kv_recv.at[d - 1, g], me + d,
        )

    def homeward(d, g):
        return remote(
            part.at[d - 1, g], back.at[d - 1, g],
            grad_send.at[d - 1, g], grad_recv.at[d - 1, g], me - d,
        )

    barrier = pltpu.get_barrier_semaphore()

    for d in distances:
        @pl.when(me + d < size)
        def _():
            pl.semaphore_signal(barrier, inc=1, device_id={"ctx": me + d}, device_id_type=MESH)

        @pl.when(me >= d)
        def _():
            pl.semaphore_signal(barrier, inc=1, device_id={"ctx": me - d}, device_id_type=MESH)

    peers = jnp.minimum(me, reach) + jnp.minimum(size - 1 - me, reach)
    pl.semaphore_wait(barrier, peers)

    @pl.loop(0, groups)
    def _(g):
        kv_all[g, 0, slot(0), :] = k_ref[g]
        kv_all[g, 1, slot(0), :] = v_ref[g]

        for d in reversed(distances):
            @pl.when(me + d < size)
            def _():
                outward(d, g).start()

    q_wide[...] = q_ref[...].astype(F32).reshape(rows * heads, dim)
    g_wide[...] = g_ref[...].astype(F32).reshape(rows * heads, dim)

    column = lax.broadcasted_iota(jnp.int32, (1, step), 1)
    at = lax.broadcasted_iota(jnp.int32, (depth, step), 0)
    for u in range(units):
        position = me * rows + u * step + column
        first = jnp.maximum(position - (WINDOW - 1), 0)
        end = jnp.int32(0)
        for n in range(doc_ref.shape[0]):
            end = end + doc_ref[n]
            first = jnp.maximum(first, jnp.where(position >= end, end, 0))
        first = first - (me - reach) * rows - u * step
        seen = (at >= first) & (at <= column + reach * rows)
        mask = jnp.where(seen, 0.0, MASKED).astype(F32)
        for n in range(per):
            bias[u, :, n * step:(n + 1) * step] = mask

    for d in distances:
        @pl.when(me < d)
        def _():
            kv_all[:, :, slot(d), :] = jnp.zeros((groups, 2, rows, dim), BF16)

    def across(left, right):
        return lax.dot_general(left, right, (((1,), (1,)), ((), ())), preferred_element_type=F32)

    def product(left, right):
        return jnp.dot(left, right, preferred_element_type=F32)

    def flipped(array):
        return array.astype(F32).T.astype(BF16)

    def head_rows(wide, g, u):
        starts = [u * step * heads + g * per + n for n in range(per)]
        return jnp.concatenate(
            [wide[pl.ds(start, step, stride=heads), :] for start in starts], 0
        ).astype(BF16)

    def finish(g):
        for d in distances:
            @pl.when(me + d < size)
            def _():
                homeward(d, g).wait_recv()
                k_own[g] += back[d - 1, g, 0].astype(F32)
                v_own[g] += back[d - 1, g, 1].astype(F32)

        dk_ref[g] = k_own[g].astype(BF16)
        dv_ref[g] = v_own[g].astype(BF16)

    @pl.loop(0, groups)
    def _(g):
        for d in distances:
            @pl.when(me >= d)
            def _():
                outward(d, g).wait_recv()

        each = range(units)
        reached = [pl.ds(u * step, depth) for u in each]
        query = [head_rows(q_wide, g, u) for u in each]
        grad = [head_rows(g_wide, g, u) for u in each]
        products = [across(kv_all[g, 0, reached[u], :], query[u]) for u in each]
        weight_grad = [across(kv_all[g, 1, reached[u], :], grad[u]) for u in each]
        key_turned, value_turned = flipped(kv_all[g, 0]), flipped(kv_all[g, 1])
        key_grad, value_grad = [], []
        for u in each:
            scores = products[u] * (SCALING * LOG2E) + bias[u]
            expo = jnp.exp2(scores - jnp.max(scores, axis=0, keepdims=True))
            inverse = 1.0 / jnp.sum(expo, axis=0, keepdims=True)
            row_total = jnp.sum(expo * weight_grad[u], axis=0, keepdims=True) * inverse
            weights = expo * inverse
            rounded = weights.astype(BF16)
            score_grad = (weights * (weight_grad[u] - row_total)).astype(BF16)
            key_grad.append(product(score_grad, query[u]) * SCALING)
            value_grad.append(product(rounded, grad[u]))
            low = u * step
            out_ref[g, u] = product(value_turned[:, low:low + depth], rounded).T.astype(BF16)
            turned = product(key_turned[:, low:low + depth], score_grad) * SCALING
            dq_ref[g, u] = turned.T.astype(BF16)

        def total(shares, low):
            found = [
                share[low - u * step:low - u * step + step]
                for u, share in enumerate(shares)
                if 0 <= low - u * step < depth
            ]
            return functools.reduce(jnp.add, found)

        for n in range(units):
            inner = slice(n * step, (n + 1) * step)
            k_own[g, inner] = total(key_grad, reach * rows + n * step)
            v_own[g, inner] = total(value_grad, reach * rows + n * step)
            for d in distances:
                low = (reach - d) * rows + n * step
                part[d - 1, g, 0, inner] = total(key_grad, low).astype(BF16)
                part[d - 1, g, 1, inner] = total(value_grad, low).astype(BF16)
        for d in reversed(distances):
            @pl.when(me >= d)
            def _():
                homeward(d, g).start()

        @pl.when(g >= LAG)
        def _():
            finish(g - LAG)

    @pl.loop(groups - LAG, groups)
    def _(g):
        finish(g)

    @pl.loop(0, groups)
    def _(g):
        for d in distances:
            @pl.when(me + d < size)
            def _():
                outward(d, g).wait_send()

            @pl.when(me >= d)
            def _():
                homeward(d, g).wait_send()


def body(queries, keys, values, out_grad, doc_lengths):
    rows, heads, dim = queries.shape
    groups = keys.shape[1]
    per = heads // groups
    step = 128
    units = rows // step
    size = lax.axis_size("ctx")
    reach = min(WINDOW, rows * size // 4) // rows
    span = (reach + 1) * rows

    def joined(array):
        array = array.reshape(groups, units, per, step, dim).transpose(1, 3, 0, 2, 4)
        return array.reshape(rows, heads, dim)

    vmem = pl.BlockSpec(memory_space=pltpu.VMEM)
    dma = pltpu.SemaphoreType.DMA((reach, groups))
    wide = jax.ShapeDtypeStruct((groups, units, per * step, dim), BF16)
    narrow = jax.ShapeDtypeStruct((groups, rows, dim), BF16)
    shares = pltpu.VMEM((reach, groups, 2, rows, dim), BF16)
    out, dq, dk, dv = pl.pallas_call(
        functools.partial(kernel, size, reach),
        out_shape=(wide, wide, narrow, narrow),
        in_specs=[pl.BlockSpec(memory_space=pltpu.SMEM)] + [vmem] * 4,
        out_specs=(vmem,) * 4,
        scratch_shapes=[
            pltpu.VMEM((rows * heads, dim), F32),
            pltpu.VMEM((rows * heads, dim), F32),
            pltpu.VMEM((groups, rows, dim), F32),
            pltpu.VMEM((groups, rows, dim), F32),
            pltpu.VMEM((groups, 2, span, dim), BF16),
            shares, shares,
            pltpu.VMEM((units, reach * rows + step, per * step), F32),
            dma, dma, dma, dma,
        ],
        compiler_params=pltpu.CompilerParams(
            collective_id=0, has_side_effects=True, vmem_limit_bytes=48 * 2**20
        ),
    )(doc_lengths, queries, out_grad, keys.transpose(1, 0, 2), values.transpose(1, 0, 2))
    return joined(out), joined(dq), dk.transpose(1, 0, 2), dv.transpose(1, 0, 2)


def solution(mesh):
    spec = P(("dp", "ctx"), "head", None)
    return jax.shard_map(
        body,
        mesh=mesh,
        in_specs=(spec, spec, spec, spec, P("dp")),
        out_specs=(spec, spec, spec, spec),
        check_vma=False,
    )
```
